256 devices in a mesh: row: 16 (over y, x), col: 16 (over z, core).
Axes of the slice: x: 4, y: 4, z: 8, core: 2. Of those that a mesh axis runs over, the one named last changes fastest.
Arguments:
- frozen_down_weight: bfloat16 [2, 12288, 28672], P(None, 'row', 'col'), may hold values from -0.0625 to 0.0625
- merged_weight_gradient: bfloat16 [2, 12288, 28672], P(None, 'row', 'col'), may hold values from -6 to 6
- adapter_up_matrix: bfloat16 [2, 12288, 64], P(None, 'row', 'col'), may hold values from -0.75 to 0.75
- adapter_down_matrix: bfloat16 [2, 64, 28672], P(None, 'row', 'col'), may hold values from -0.3125 to 0.3125
- magnitude: float32 [2, 28672], P(None, 'col'), may hold values from 0.5 to 2
Outputs:
- grad_b: float32 [2, 12288, 64], P(None, 'row', 'col')
- grad_a: float32 [2, 64, 28672], P(None, 'row', 'col')
- grad_mag: float32 [2, 28672], P(None, 'col')
The draws below stay inside these ranges and needn't reach their ends.
All inputs are finite; a program needn't handle non-finite values.
Results may differ from the reference program's by a relative error of at most 0.0025.
Values may be sent and summed in bfloat16 or wider, within the bound.
No kernel may reach another device: no remote copies, remote signals or barrier semaphores. Data moves between devices by JAX's collectives and lax.ppermute only.
A program may use at most 64 MiB of HBM per device.

```python
import math
import jax
import jax.numpy as jnp
from jax import lax

OUTPUT_FEATURES = 12288
INPUT_FEATURES = 28672
ADAPTER_RANK = 64
LAYER_COUNT = 2
N_COL = 16


def shared_fields(key, spread):
    key_normal = jax.random.fold_in(key, 0)
    key_rows = jax.random.fold_in(key, 2)
    key_cols = jax.random.fold_in(key, 3)
    full_shape = (LAYER_COUNT, OUTPUT_FEATURES, INPUT_FEATURES)
    base = jax.random.normal(key_normal, full_shape, jnp.float32)
    rows = jnp.arange(OUTPUT_FEATURES, dtype=jnp.float32).reshape(1, OUTPUT_FEATURES, 1)
    rising = 1.0 + 2.0 * rows / max(OUTPUT_FEATURES - 1, 1)
    row_scale = rising * jnp.exp(spread * jax.random.uniform(key_rows, (LAYER_COUNT, OUTPUT_FEATURES, 1), jnp.float32))
    col_scale = jnp.exp(spread * jax.random.uniform(key_cols, (LAYER_COUNT, 1, INPUT_FEATURES), jnp.float32))
    return (base, row_scale, col_scale)


def draw_frozen_down_weight(key, part):
    base, row_scale, col_scale = shared_fields(key, math.log(10.0))
    values = base * row_scale * col_scale / (10.0 * math.sqrt(OUTPUT_FEATURES))
    return jnp.clip(values, -0.0625, 0.0625).astype(jnp.bfloat16)


def draw_merged_weight_gradient(key, part):
    base, row_scale, col_scale = shared_fields(key, math.log(10.0))
    key = jax.random.fold_in(key, 23)
    noise = jax.random.normal(key, (LAYER_COUNT, OUTPUT_FEATURES, INPUT_FEATURES), jnp.float32)
    values = 0.01 * base * row_scale + noise
    return jnp.clip(values, -6.0, 6.0).astype(jnp.bfloat16)


def block_scale(key, shape, cuts, low, largest):
    factor_of = 1.0
    for axis_at, parts in cuts:
        heights = jax.random.uniform(jax.random.fold_in(jax.random.fold_in(key, 6), axis_at), (parts,), jnp.float32, low / len(cuts), largest / len(cuts))
        factor_of = factor_of * jnp.repeat(jnp.exp(heights), shape[axis_at] // parts).reshape((-1,) + (1,) * (len(shape) - 1 - axis_at))
    return factor_of


def bell_draw(key, dims, scale, limit, cuts=(), kind=jnp.bfloat16):
    result = scale * jax.random.normal(key, dims, jnp.float32)
    if cuts:
        result = result * block_scale(key, dims, cuts, -0.22, 0.18)
    return jnp.clip(result, -limit, limit).astype(kind)


def setup_inputs(seed: int = 0) -> dict:
    streams_of = jax.random.split(jax.random.key(seed), 6)
    return {
        "frozen_down_weight": draw_frozen_down_weight(jax.random.fold_in(streams_of[5], 71), 0),
        "merged_weight_gradient": draw_merged_weight_gradient(jax.random.fold_in(streams_of[5], 71), 0),
        "adapter_up_matrix": bell_draw(streams_of[2], (LAYER_COUNT, OUTPUT_FEATURES, ADAPTER_RANK), 0.05, 0.75, ((1, 16), (2, 16))),
        "adapter_down_matrix": bell_draw(streams_of[3], (LAYER_COUNT, ADAPTER_RANK, INPUT_FEATURES), 0.02, 0.3125, ((1, 16), (2, 16))),
        "magnitude": jnp.clip(jnp.exp(math.log(2.0) - 1.3862944 * jax.random.uniform(streams_of[4], (LAYER_COUNT, INPUT_FEATURES), jnp.float32) ** block_scale(streams_of[4], (LAYER_COUNT, INPUT_FEATURES), ((1, 16),), -0.2, 0.2)), 0.5, 2.0),
    }


epsilon = 1e-06

def coefficients(squares, inner, magnitude):
    norm = jnp.sqrt(squares + epsilon)
    scale = magnitude / norm
    shrink = scale * inner / (norm * norm)
    return (scale, shrink, inner / norm)

def per_layer_gradients(weight, cotangent, left, right, magnitude):
    width = INPUT_FEATURES // N_COL

    def block_step(total, index):
        start = (index * width).astype(jnp.int32)
        weight_block = lax.dynamic_slice_in_dim(weight, start, width, 1)
        cot_block = lax.dynamic_slice_in_dim(cotangent, start, width, 1)
        right_block = lax.dynamic_slice_in_dim(right, start, width, 1)
        mag_block = lax.dynamic_slice_in_dim(magnitude, start, width, 0)
        merged = weight_block.astype(jnp.float32) + jnp.dot(left, right_block, preferred_element_type=jnp.float32)
        cot_float = cot_block.astype(jnp.float32)
        squares = lax.optimization_barrier(jnp.sum(merged * merged, axis=0))
        inner = lax.optimization_barrier(jnp.sum(cot_float * merged, axis=0))
        scale, shrink, magnitude_gradient = coefficients(squares, inner, mag_block)
        grad_merged = (scale * cot_float - shrink * merged).astype(jnp.bfloat16)
        total = total + jnp.dot(grad_merged, right_block.T, preferred_element_type=jnp.float32)
        right_factor_gradient = jnp.dot(left.T, grad_merged, preferred_element_type=jnp.float32)
        return (total, (magnitude_gradient, right_factor_gradient))
    start_total = jnp.zeros((OUTPUT_FEATURES, ADAPTER_RANK), jnp.float32)
    left_factor_gradient, (mag_grads, right_grads) = lax.scan(block_step, start_total, jnp.arange(N_COL, dtype=jnp.int32))
    magnitude_gradient = mag_grads.reshape(INPUT_FEATURES)
    right_factor_gradient = jnp.transpose(right_grads, (1, 0, 2)).reshape(ADAPTER_RANK, INPUT_FEATURES)
    return (left_factor_gradient, right_factor_gradient, magnitude_gradient)

def reference(frozen_down_weight, merged_weight_gradient, adapter_up_matrix, adapter_down_matrix, magnitude):
    lefts = []
    rights = []
    mags = []
    for layer_position in range(LAYER_COUNT):
        left_factor_gradient, right_factor_gradient, magnitude_gradient = per_layer_gradients(frozen_down_weight[layer_position], merged_weight_gradient[layer_position], adapter_up_matrix[layer_position], adapter_down_matrix[layer_position], magnitude[layer_position])
        lefts.append(left_factor_gradient)
        rights.append(right_factor_gradient)
        mags.append(magnitude_gradient)
    return (jnp.stack(lefts), jnp.stack(rights), jnp.stack(mags))
```

```python
import functools

import jax
import jax.numpy as jnp
from jax import lax
from jax.experimental import pallas as pl
from jax.experimental.pallas import tpu as pltpu
from jax.sharding import PartitionSpec as P

epsilon = 1e-06
LAYERS = 2
SIDE = 4
GROUPS = SIDE * SIDE
RANKS_HERE = 4
SLAB = LAYERS * RANKS_HERE
DEPTH = GROUPS * SLAB
BLOCK = 256
VMEM_BYTES = 48 * 1024 * 1024


def shift_x(k):
    return [(y * SIDE + x, y * SIDE + (x + k) % SIDE) for y in range(SIDE) for x in range(SIDE)]


def shift_y(k):
    return [(y * SIDE + x, (y + k) % SIDE * SIDE + x) for y in range(SIDE) for x in range(SIDE)]


def group_at(me, ky, kx):
    y, x = me // SIDE, me % SIDE
    return (y + SIDE - ky) % SIDE * SIDE + (x + SIDE - kx) % SIDE


def layer_mask(layer, shape):
    row = lax.broadcasted_iota(jnp.int32, shape, 0)
    return (row // RANKS_HERE) % LAYERS == layer


def sums_kernel(me_ref, w_ref, g_ref, b_ref, a0, a1, a2, a3, s_ref, bz_ref, bt_ref, order):
    @pl.when(pl.program_id(0) == 0)
    def _():
        me = me_ref[0]
        for ky in range(SIDE):
            for kx in range(SIDE):
                at = (ky * SIDE + kx) * SLAB
                order[at : at + SLAB, :] = b_ref[group_at(me, ky, kx)].astype(jnp.float32)
        for layer in range(LAYERS):
            masked = jnp.where(layer_mask(layer, order.shape), order[...], 0.0)
            bz_ref[layer] = masked.astype(jnp.bfloat16)
            bt_ref[layer] = masked.T.astype(jnp.bfloat16)

    a = jnp.concatenate([a0[...], a1[...], a2[...], a3[...]], axis=0)
    rows = []
    for layer in range(LAYERS):
        merged = w_ref[layer].astype(jnp.float32) + jnp.dot(
            bt_ref[layer], a, preferred_element_type=jnp.float32
        )
        cot = g_ref[layer].astype(jnp.float32)
        rows.append(jnp.sum(merged * merged, axis=0, keepdims=True))
        rows.append(jnp.sum(cot * merged, axis=0, keepdims=True))
    sums = jnp.concatenate(rows, axis=0)
    s_ref[...] = jnp.broadcast_to(sums[None], s_ref.shape)


def grads_kernel(
    me_ref, w_ref, g_ref, bz_ref, bt_ref, a0, a1, a2, a3, s_ref, mag_ref,
    x0, x1, x2, x3, tb_ref, gmag_ref, total,
):
    step = pl.program_id(0)
    a = jnp.concatenate([a0[...], a1[...], a2[...], a3[...]], axis=0)
    a_wide = a.astype(jnp.float32)
    sums = jnp.sum(s_ref[...], axis=0)
    term_a = None
    term_b = None
    for layer in range(LAYERS):
        squares = sums[2 * layer : 2 * layer + 1]
        inner = sums[2 * layer + 1 : 2 * layer + 2]
        norm = jnp.sqrt(squares + epsilon)
        scale = mag_ref[layer : layer + 1, :] / norm
        shrink = scale * inner / (norm * norm)
        gmag_ref[layer : layer + 1, :] = inner / norm
        merged = w_ref[layer].astype(jnp.float32) + jnp.dot(
            bt_ref[layer], a, preferred_element_type=jnp.float32
        )
        cot = g_ref[layer].astype(jnp.float32)
        grad = (scale * cot - shrink * merged).astype(jnp.bfloat16)
        az = jnp.where(layer_mask(layer, a_wide.shape), a_wide, 0.0).astype(jnp.bfloat16)
        part_a = jnp.dot(bz_ref[layer], grad, preferred_element_type=jnp.float32)
        part_b = lax.dot_general(
            az, grad, (((1,), (1,)), ((), ())), preferred_element_type=jnp.float32
        )
        term_a = part_a if term_a is None else term_a + part_a
        term_b = part_b if term_b is None else term_b + part_b
    for kx, out in enumerate((x0, x1, x2, x3)):
        for ky in range(SIDE):
            at = (ky * SIDE + kx) * SLAB
            out[ky] = term_a[at : at + SLAB]

    @pl.when(step == 0)
    def _():
        total[...] = term_b

    @pl.when(step > 0)
    def _():
        total[...] += term_b

    @pl.when(step == pl.num_programs(0) - 1)
    def _():
        me = me_ref[0]
        for ky in range(SIDE):
            for kx in range(SIDE):
                at = (ky * SIDE + kx) * SLAB
                tb_ref[group_at(me, ky, kx)] = total[at : at + SLAB]


def whole(shape):
    return pl.BlockSpec(shape, lambda c, me: (0,) * len(shape))


def columns(shape):
    return pl.BlockSpec(shape, lambda c, me: (0,) * (len(shape) - 1) + (c,))


def on_device(weight, cotangent, up, down, magnitude):
    layers, height, width = weight.shape
    steps = width // BLOCK
    me = lax.axis_index("row").astype(jnp.int32).reshape(1)

    up_slab = jnp.swapaxes(up, 1, 2).reshape(SLAB, height)
    up_all = lax.all_to_all(jnp.broadcast_to(up_slab, (GROUPS, SLAB, height)), "col", 0, 0)

    along_x = [down] + [lax.ppermute(down, "row", shift_x(k)) for k in range(1, SIDE)]
    down_x = jnp.stack(along_x).reshape(SIDE * SLAB, width)
    downs = [down_x] + [lax.ppermute(down_x, "row", shift_y(k)) for k in range(1, SIDE)]

    params = pltpu.CompilerParams(vmem_limit_bytes=VMEM_BYTES)
    down_specs = [columns((SIDE * SLAB, BLOCK))] * SIDE
    sums, up_rows, up_columns = pl.pallas_call(
        sums_kernel,
        grid_spec=pltpu.PrefetchScalarGridSpec(
            num_scalar_prefetch=1,
            grid=(steps,),
            in_specs=[
                columns((layers, height, BLOCK)),
                columns((layers, height, BLOCK)),
                whole((GROUPS, SLAB, height)),
                *down_specs,
            ],
            out_specs=[
                columns((GROUPS, 2 * layers, BLOCK)),
                whole((layers, DEPTH, height)),
                whole((layers, height, DEPTH)),
            ],
            scratch_shapes=[pltpu.VMEM((DEPTH, height), jnp.float32)],
        ),
        out_shape=[
            jax.ShapeDtypeStruct((GROUPS, 2 * layers, width), jnp.float32),
            jax.ShapeDtypeStruct((layers, DEPTH, height), jnp.bfloat16),
            jax.ShapeDtypeStruct((layers, height, DEPTH), jnp.bfloat16),
        ],
        compiler_params=params,
        name="column_sums",
    )(me, weight, cotangent, up_all, *downs)

    sums_all = lax.all_to_all(sums, "row", 0, 0)

    *terms_x, term_b, mags = pl.pallas_call(
        grads_kernel,
        grid_spec=pltpu.PrefetchScalarGridSpec(
            num_scalar_prefetch=1,
            grid=(steps,),
            in_specs=[
                columns((layers, height, BLOCK)),
                columns((layers, height, BLOCK)),
                whole((layers, DEPTH, height)),
                whole((layers, height, DEPTH)),
                *down_specs,
                columns((GROUPS, 2 * layers, BLOCK)),
                columns((layers, BLOCK)),
            ],
            out_specs=[
                *[columns((SIDE, SLAB, BLOCK))] * SIDE,
                whole((GROUPS, SLAB, height)),
                columns((layers, BLOCK)),
            ],
            scratch_shapes=[pltpu.VMEM((DEPTH, height), jnp.float32)],
        ),
        out_shape=[
            *[jax.ShapeDtypeStruct((SIDE, SLAB, width), jnp.float32)] * SIDE,
            jax.ShapeDtypeStruct((GROUPS, SLAB, height), jnp.float32),
            jax.ShapeDtypeStruct((layers, width), jnp.float32),
        ],
        compiler_params=params,
        name="gradients",
    )(me, weight, cotangent, up_rows, up_columns, *downs, sums_all, magnitude)

    parts_b = lax.all_to_all(term_b, "col", 0, 0)
    sum_x = terms_x[0]
    for k in range(1, SIDE):
        sum_x = sum_x + lax.ppermute(terms_x[k], "row", shift_x(-k))
    sum_y = sum_x[0]
    for k in range(1, SIDE):
        sum_y = sum_y + lax.ppermute(sum_x[k], "row", shift_y(-k))
    grad_b = jnp.sum(parts_b, axis=0).reshape(layers, RANKS_HERE, height)
    return jnp.swapaxes(grad_b, 1, 2), sum_y.reshape(layers, RANKS_HERE, width), mags


def solution(mesh):
    in_specs = (
        P(None, "row", "col"),
        P(None, "row", "col"),
        P(None, "row", "col"),
        P(None, "row", "col"),
        P(None, "col"),
    )
    out_specs = (P(None, "row", "col"), P(None, "row", "col"), P(None, "col"))
    return jax.shard_map(
        on_device, mesh=mesh, in_specs=in_specs, out_specs=out_specs, check_vma=False
    )
```

```python
import jax
import jax.numpy as jnp
from jax import lax
from jax.experimental import pallas as pl
from jax.experimental.pallas import tpu as pltpu
from jax.sharding import PartitionSpec as P

epsilon = 1e-06
LAYERS = 2
GROUPS = 16
RANKS_HERE = 4
SLAB = LAYERS * RANKS_HERE
DEPTH = GROUPS * SLAB
SIDE = 4
RING = 8
REACH = RING // 2
BLOCK = 256
VMEM_BYTES = 20 * 1024 * 1024
IN_VMEM = pl.BlockSpec(memory_space=pltpu.VMEM)
IN_SMEM = pl.BlockSpec(memory_space=pltpu.SMEM)

SWAP_CORE = [(i, i ^ 1) for i in range(GROUPS)]


def z_apart(k):
    ahead = [(2 * z, (z + k) % RING * 2) for z in range(RING)]
    behind = [(2 * z + 1, (z + RING - k) % RING * 2 + 1) for z in range(RING)]
    return ahead if k == REACH else ahead + behind


def x_shift(k):
    return [(y * SIDE + x, y * SIDE + (x + k) % SIDE) for y in range(SIDE) for x in range(SIDE)]


def y_shift(k):
    return [(y * SIDE + x, (y + k) % SIDE * SIDE + x) for y in range(SIDE) for x in range(SIDE)]


def col_group(col, core_sign, k, swap):
    core = col % 2
    step = core_sign * (1 - 2 * core) * k
    return (col // 2 + RING + step) % RING * 2 + (core + swap) % 2


def row_group(row, ky, kx):
    return (row // SIDE + SIDE - ky) % SIDE * SIDE + (row % SIDE + SIDE - kx) % SIDE


def layer_mask(layer, shape):
    row = lax.broadcasted_iota(jnp.int32, shape, 0)
    return (row // RANKS_HERE) % LAYERS == layer


def stack_kernel(d0, d1, d2, d3, out_ref):
    rows = [d[layer].astype(jnp.float32) for d in (d0, d1, d2, d3) for layer in range(LAYERS)]
    out_ref[...] = jnp.concatenate(rows, axis=0).astype(jnp.bfloat16)


def sums_kernel(
    me_ref, w_ref, g_ref, pair, mine, theirs, a0, a1, a2, a3, s_ref, bz_ref, bt_ref, found, order
):
    row, col = me_ref[0], me_ref[1]

    def put(group, slab):
        for layer in range(LAYERS):
            found[group, layer * RANKS_HERE : (layer + 1) * RANKS_HERE, :] = slab[layer].astype(jnp.float32)

    for swap in range(2):
        put(col_group(col, 1, 0, swap), pair[swap])
        for k in range(1, REACH):
            put(col_group(col, -1, k, swap), mine[k - 1, swap])
            put(col_group(col, 1, k, 1 - swap), theirs[k - 1, swap])
        far = mine[REACH - 1, swap].astype(jnp.float32) + theirs[REACH - 1, 1 - swap].astype(jnp.float32)
        put(col_group(col, -1, REACH, swap), far)
    for ky in range(SIDE):
        for kx in range(SIDE):
            order[ky * SIDE + kx] = found[row_group(row, ky, kx)]
    here, there = (x[...].reshape(bz_ref.shape[1:]) for x in (found, order))
    for layer in range(LAYERS):
        mask = layer_mask(layer, here.shape)
        bz_ref[layer] = jnp.where(mask, here, 0.0).astype(jnp.bfloat16)
        bt_ref[layer] = jnp.where(mask, there, 0.0).T.astype(jnp.bfloat16)

    for start in range(0, w_ref.shape[2], BLOCK):
        here = pl.ds(start, BLOCK)
        a = jnp.concatenate([x[:, here] for x in (a0, a1, a2, a3)], axis=0)
        rows = []
        for layer in range(LAYERS):
            merged = w_ref[layer, :, here].astype(jnp.float32) + jnp.dot(
                bt_ref[layer], a, preferred_element_type=jnp.float32
            )
            cot = g_ref[layer, :, here].astype(jnp.float32)
            rows.append(jnp.sum(merged * merged, axis=0, keepdims=True))
            rows.append(jnp.sum(cot * merged, axis=0, keepdims=True))
        sums = jnp.concatenate(rows, axis=0)
        s_ref[:, :, here] = jnp.broadcast_to(sums[None], (GROUPS, 2 * LAYERS, BLOCK))


def grads_kernel(
    me_ref, w_ref, g_ref, bz_ref, bt_ref, a0, a1, a2, a3, s_ref, mag_ref,
    ta_ref, self_ref, keep_ref, send_ref, gmag_ref, total,
):
    for start in range(0, w_ref.shape[2], BLOCK):
        here = pl.ds(start, BLOCK)
        a = jnp.concatenate([x[:, here] for x in (a0, a1, a2, a3)], axis=0)
        a_wide = a.astype(jnp.float32)
        sums = jnp.sum(s_ref[:, :, here], axis=0)
        term_a = None
        term_b = None
        for layer in range(LAYERS):
            squares = sums[2 * layer : 2 * layer + 1]
            inner = sums[2 * layer + 1 : 2 * layer + 2]
            norm = jnp.sqrt(squares + epsilon)
            scale = mag_ref[layer : layer + 1, here] / norm
            shrink = scale * inner / (norm * norm)
            gmag_ref[layer : layer + 1, here] = inner / norm
            merged = w_ref[layer, :, here].astype(jnp.float32) + jnp.dot(
                bt_ref[layer], a, preferred_element_type=jnp.float32
            )
            cot = g_ref[layer, :, here].astype(jnp.float32)
            grad = (scale * cot - shrink * merged).astype(jnp.bfloat16)
            az = jnp.where(layer_mask(layer, a_wide.shape), a_wide, 0.0).astype(jnp.bfloat16)
            part_a = jnp.dot(bz_ref[layer], grad, preferred_element_type=jnp.float32)
            part_b = lax.dot_general(
                az, grad, (((1,), (1,)), ((), ())), preferred_element_type=jnp.float32
            )
            term_a = part_a if term_a is None else term_a + part_a
            term_b = part_b if term_b is None else term_b + part_b
        ta_ref[:, :, here] = term_a.reshape(GROUPS, SLAB, BLOCK)
        term_b = term_b.reshape(total.shape)
        if start == 0:
            total[...] = term_b
        else:
            total[...] += term_b
    row, col = me_ref[0], me_ref[1]

    def sum_for(group):
        ky = (row // SIDE + SIDE - group // SIDE) % SIDE
        kx = (row % SIDE + SIDE - group % SIDE) % SIDE
        return total[ky * SIDE + kx]

    for swap in range(2):
        self_ref[swap] = sum_for(col_group(col, 1, 0, swap))
        for k in range(1, REACH + 1):
            keep_ref[k - 1, swap] = sum_for(col_group(col, 1, k, swap))
            send_ref[k - 1, swap] = sum_for(col_group(col, -1, k, 1 - swap))


def on_device(weight, cotangent, up, down, magnitude):
    layers, height, width = weight.shape
    me = jnp.stack([lax.axis_index("row"), lax.axis_index("col")]).astype(jnp.int32)
    params = pltpu.CompilerParams(vmem_limit_bytes=VMEM_BYTES)

    up = jnp.swapaxes(up, 1, 2)
    pair = jnp.stack([up, lax.ppermute(up, "col", SWAP_CORE)])
    mine = jnp.stack([lax.ppermute(pair, "col", z_apart(k)) for k in range(1, REACH + 1)])
    theirs = lax.ppermute(mine, "col", SWAP_CORE)

    near = [down] + [lax.ppermute(down, "row", x_shift(k)) for k in range(1, SIDE)]
    near = pl.pallas_call(
        stack_kernel,
        in_specs=[IN_VMEM] * SIDE,
        out_specs=IN_VMEM,
        out_shape=jax.ShapeDtypeStruct((SIDE * SLAB, width), down.dtype),
        compiler_params=params,
        cost_estimate=pl.CostEstimate(flops=10**10, bytes_accessed=10**6, transcendentals=0),
        name="stack",
    )(*near)
    downs = [near] + [lax.ppermute(near, "row", y_shift(k)) for k in range(1, SIDE)]

    sums, up_rows, up_columns = pl.pallas_call(
        sums_kernel,
        in_specs=[IN_SMEM] + [IN_VMEM] * 9,
        out_specs=[IN_VMEM] * 3,
        out_shape=[
            jax.ShapeDtypeStruct((GROUPS, 2 * layers, width), jnp.float32),
            jax.ShapeDtypeStruct((layers, DEPTH, height), jnp.bfloat16),
            jax.ShapeDtypeStruct((layers, height, DEPTH), jnp.bfloat16),
        ],
        scratch_shapes=[pltpu.VMEM((GROUPS, SLAB, height), jnp.float32)] * 2,
        compiler_params=params,
        name="column_sums",
    )(me, weight, cotangent, pair, mine, theirs, *downs)

    sums_all = lax.all_to_all(sums, "row", 0, 0)

    term_a, self_b, keep_b, send_b, mags = pl.pallas_call(
        grads_kernel,
        in_specs=[IN_SMEM] + [IN_VMEM] * 10,
        out_specs=[IN_VMEM] * 5,
        out_shape=[
            jax.ShapeDtypeStruct((GROUPS, SLAB, width), jnp.float32),
            jax.ShapeDtypeStruct((2, SLAB, height), jnp.float32),
            *[jax.ShapeDtypeStruct((REACH, 2, SLAB, height), jnp.float32)] * 2,
            jax.ShapeDtypeStruct((layers, width), jnp.float32),
        ],
        scratch_shapes=[pltpu.VMEM((GROUPS, SLAB, height), jnp.float32)],
        compiler_params=params,
        name="gradients",
    )(me, weight, cotangent, up_rows, up_columns, *downs, sums_all, magnitude)

    sum_core = keep_b + lax.ppermute(send_b, "col", SWAP_CORE)
    for k in range(1, REACH + 1):
        self_b = self_b + lax.ppermute(sum_core[k - 1], "col", z_apart(k))
    grad_b = self_b[0] + lax.ppermute(self_b[1], "col", SWAP_CORE)

    grad_a = jnp.sum(lax.all_to_all(term_a, "row", 0, 0), axis=0)
    grad_b = grad_b.reshape(layers, RANKS_HERE, height)
    return jnp.swapaxes(grad_b, 1, 2), grad_a.reshape(layers, RANKS_HERE, width), mags


def solution(mesh):
    in_specs = (
        P(None, "row", "col"),
        P(None, "row", "col"),
        P(None, "row", "col"),
        P(None, "row", "col"),
        P(None, "col"),
    )
    out_specs = (P(None, "row", "col"), P(None, "row", "col"), P(None, "col"))
    return jax.shard_map(
        on_device, mesh=mesh, in_specs=in_specs, out_specs=out_specs, check_vma=False
    )
```

```python
import jax
import jax.numpy as jnp
from jax import lax
from jax.experimental import pallas as pl
from jax.experimental.pallas import tpu as pltpu
from jax.sharding import PartitionSpec as P

epsilon = 1e-06
LAYERS = 2
GROUPS = 16
RANKS_HERE = 4
SLAB = LAYERS * RANKS_HERE
DEPTH = GROUPS * SLAB
SIDE = 4
RING = 8
REACH = RING // 2
BLOCK = 256
VMEM_BYTES = 20 * 1024 * 1024
IN_VMEM = pl.BlockSpec(memory_space=pltpu.VMEM)
ANYWHERE = pl.BlockSpec(memory_space=pl.ANY)
IN_SMEM = pl.BlockSpec(memory_space=pltpu.SMEM)

SWAP_CORE = [(i, i ^ 1) for i in range(GROUPS)]


def z_apart(k):
    ahead = [(2 * z, (z + k) % RING * 2) for z in range(RING)]
    behind = [(2 * z + 1, (z + RING - k) % RING * 2 + 1) for z in range(RING)]
    return ahead + behind


SEEN = [(1, 0), (1, 1), (2, 0), (2, 1), (3, 0), (3, 1), (REACH, 0), (0, 0)]


def row_shift(k, second):
    pairs = []
    for row in range(GROUPS):
        y, x = row // SIDE, row % SIDE
        for col in range(GROUPS):
            along_y = (col % 2 + second) % 2
            to = (y + k) % SIDE * SIDE + x if along_y else y * SIDE + (x + k) % SIDE
            pairs.append((row * GROUPS + col, to * GROUPS + col))
    return pairs


def col_group(col, core_sign, k, swap):
    core = col % 2
    step = core_sign * (1 - 2 * core) * k
    return (col // 2 + RING + step) % RING * 2 + (core + swap) % 2


def row_group(row, col, second, first):
    core = col % 2
    ky = second * (1 - core) + first * core
    kx = first * (1 - core) + second * core
    return (row // SIDE + SIDE - ky) % SIDE * SIDE + (row % SIDE + SIDE - kx) % SIDE


def row_place(row, col, group):
    core = col % 2
    ky = (row // SIDE + SIDE - group // SIDE) % SIDE
    kx = (row % SIDE + SIDE - group % SIDE) % SIDE
    return (ky * (1 - core) + kx * core) * SIDE + kx * (1 - core) + ky * core


def layer_mask(layer, shape):
    row = lax.broadcasted_iota(jnp.int32, shape, 0)
    return (row // RANKS_HERE) % LAYERS == layer


def stack_kernel(d0, d1, d2, d3, out_ref):
    rows = [d[layer].astype(jnp.float32) for d in (d0, d1, d2, d3) for layer in range(LAYERS)]
    out_ref[...] = jnp.concatenate(rows, axis=0).astype(jnp.bfloat16)


def sums_kernel(
    me_ref, w_ref, g_ref, pair, mine, theirs, a0, a1, a2, a3, s_ref, bz_ref, bt_ref, found, order
):
    row, col = me_ref[0], me_ref[1]

    def put(group, slab):
        for layer in range(LAYERS):
            found[group, layer * RANKS_HERE : (layer + 1) * RANKS_HERE, :] = slab[layer].astype(jnp.float32)

    for at, (k, swap) in enumerate(SEEN[:-1]):
        put(col_group(col, -1, k, swap), mine[at])
        put(col_group(col, 1, k, 1 - swap), theirs[at])
    for swap in range(2):
        put(col_group(col, 1, 0, swap), pair[swap])
    for second in range(SIDE):
        for first in range(SIDE):
            order[second * SIDE + first] = found[row_group(row, col, second, first)]
    here, there = (x[...].reshape(DEPTH, found.shape[2]) for x in (found, order))
    for layer in range(LAYERS):
        mask = layer_mask(layer, here.shape)
        span = pl.ds(layer * found.shape[2], found.shape[2])
        bz_ref[:, span] = jnp.where(mask, here, 0.0).astype(jnp.bfloat16)
        bt_ref[layer] = jnp.where(mask, there, 0.0).T.astype(jnp.bfloat16)

    for start in range(0, w_ref.shape[2], BLOCK):
        here = pl.ds(start, BLOCK)
        a = jnp.concatenate([x[:, here] for x in (a0, a1, a2, a3)], axis=0)
        rows = []
        for layer in range(LAYERS):
            merged = w_ref[layer, :, here].astype(jnp.float32) + jnp.dot(
                bt_ref[layer], a, preferred_element_type=jnp.float32
            )
            cot = g_ref[layer, :, here].astype(jnp.float32)
            rows.append(jnp.sum(merged * merged, axis=0, keepdims=True))
            rows.append(jnp.sum(cot * merged, axis=0, keepdims=True))
        sums = jnp.concatenate(rows, axis=0)
        s_ref[:, :, here] = jnp.broadcast_to(sums[None], (GROUPS, 2 * LAYERS, BLOCK))


def grads_kernel(
    me_ref, w_ref, g_ref, bz_ref, bt_ref, a0, a1, a2, a3, s_ref, mag_ref,
    ta_ref, keep_ref, send_ref, gmag_ref, total,
):
    for start in range(0, w_ref.shape[2], BLOCK):
        here = pl.ds(start, BLOCK)
        a = jnp.concatenate([x[:, here] for x in (a0, a1, a2, a3)], axis=0)
        a_wide = a.astype(jnp.float32)
        sums = jnp.sum(s_ref[:, :, here], axis=0)
        grads = []
        factors = []
        for layer in range(LAYERS):
            squares = sums[2 * layer : 2 * layer + 1]
            inner = sums[2 * layer + 1 : 2 * layer + 2]
            norm = jnp.sqrt(squares + epsilon)
            scale = mag_ref[layer : layer + 1, here] / norm
            shrink = scale * inner / (norm * norm)
            gmag_ref[layer : layer + 1, here] = inner / norm
            merged = w_ref[layer, :, here].astype(jnp.float32) + jnp.dot(
                bt_ref[layer], a, preferred_element_type=jnp.float32
            )
            cot = g_ref[layer, :, here].astype(jnp.float32)
            grad = (scale * cot - shrink * merged).astype(jnp.bfloat16)
            az = jnp.where(layer_mask(layer, a_wide.shape), a_wide, 0.0).astype(jnp.bfloat16)
            grads.append(grad)
            factors.append(az)
        term_a = jnp.dot(
            bz_ref[...], jnp.concatenate(grads, axis=0), preferred_element_type=jnp.float32
        )
        ta_ref[:, :, here] = term_a.reshape(GROUPS, SLAB, BLOCK)
        term_b = lax.dot_general(
            jnp.concatenate(factors, axis=1),
            jnp.concatenate(grads, axis=1),
            (((1,), (1,)), ((), ())),
            preferred_element_type=jnp.float32,
        )
        term_b = term_b.reshape(total.shape)
        if start == 0:
            total[...] = term_b
        else:
            total[...] += term_b
    row, col = me_ref[0], me_ref[1]

    def sum_for(group):
        return total[row_place(row, col, group)]

    for at, (k, swap) in enumerate(SEEN):
        keep_ref[at] = sum_for(col_group(col, 1, k, swap))
        send_ref[at] = sum_for(col_group(col, -1, k, 1 - swap))


def combine_kernel(keep_ref, got_ref, one_ref, two_ref, three_ref, four_ref, here_ref):
    for k, ref in enumerate((one_ref, two_ref, three_ref)):
        ref[...] = keep_ref[2 * k : 2 * k + 2] + got_ref[2 * k : 2 * k + 2]
    four_ref[...] = keep_ref[6] + got_ref[6]
    here_ref[...] = keep_ref[7] + got_ref[7]


def finish_kernel(parts_ref, here_ref, got_ref, other_ref, ga_ref, gb_ref):
    sum_a = jnp.sum(parts_ref[...], axis=0)
    sum_b = here_ref[...] + got_ref[0] + other_ref[...]
    for layer in range(LAYERS):
        rows = slice(layer * RANKS_HERE, (layer + 1) * RANKS_HERE)
        ga_ref[layer] = sum_a[rows]
        gb_ref[layer] = sum_b[rows]


def on_device(weight, cotangent, up, down, magnitude):
    layers, height, width = weight.shape
    me = jnp.stack([lax.axis_index("row"), lax.axis_index("col")]).astype(jnp.int32)
    params = pltpu.CompilerParams(vmem_limit_bytes=VMEM_BYTES)

    up = jnp.swapaxes(up, 1, 2)
    pair = jnp.stack([up, lax.ppermute(up, "col", SWAP_CORE)])
    two = lax.ppermute(pair, "col", z_apart(2))
    one, three = (lax.ppermute(pair, "col", z_apart(k)) for k in (1, 3))
    four = lax.ppermute(two[0], "col", z_apart(2))
    mine = jnp.concatenate([one, two, three, four[None]])
    theirs = lax.ppermute(mine, "col", SWAP_CORE)

    near = [down] + [lax.ppermute(down, ("row", "col"), row_shift(k, 0)) for k in range(1, SIDE)]
    near = pl.pallas_call(
        stack_kernel,
        in_specs=[IN_VMEM] * SIDE,
        out_specs=IN_VMEM,
        out_shape=jax.ShapeDtypeStruct((SIDE * SLAB, width), down.dtype),
        compiler_params=params,
        cost_estimate=pl.CostEstimate(flops=10**10, bytes_accessed=10**6, transcendentals=0),
        name="stack",
    )(*near)
    downs = [near] + [lax.ppermute(near, ("row", "col"), row_shift(k, 1)) for k in range(1, SIDE)]

    sums, up_rows, up_columns = pl.pallas_call(
        sums_kernel,
        in_specs=[IN_SMEM] + [IN_VMEM] * 9,
        out_specs=[IN_VMEM] * 3,
        out_shape=[
            jax.ShapeDtypeStruct((GROUPS, 2 * layers, width), jnp.float32),
            jax.ShapeDtypeStruct((DEPTH, layers * height), jnp.bfloat16),
            jax.ShapeDtypeStruct((layers, height, DEPTH), jnp.bfloat16),
        ],
        scratch_shapes=[pltpu.VMEM((GROUPS, SLAB, height), jnp.float32)] * 2,
        compiler_params=params,
        name="column_sums",
    )(me, weight, cotangent, pair, mine, theirs, *downs)

    sums_all = lax.all_to_all(sums, "row", 0, 0)

    term_a, keep_b, send_b, mags = pl.pallas_call(
        grads_kernel,
        in_specs=[IN_SMEM] + [IN_VMEM] * 10,
        out_specs=[IN_VMEM] * 4,
        out_shape=[
            jax.ShapeDtypeStruct((GROUPS, SLAB, width), jnp.float32),
            *[jax.ShapeDtypeStruct((len(SEEN), SLAB, height), jnp.float32)] * 2,
            jax.ShapeDtypeStruct((layers, width), jnp.float32),
        ],
        scratch_shapes=[pltpu.VMEM((GROUPS, SLAB, height), jnp.float32)],
        compiler_params=params,
        name="gradients",
    )(me, weight, cotangent, up_rows, up_columns, *downs, sums_all, magnitude)

    pair_of = jax.ShapeDtypeStruct((2, SLAB, height), jnp.float32)
    one_of = jax.ShapeDtypeStruct((SLAB, height), jnp.float32)
    one, two, three, four, here_b = pl.pallas_call(
        combine_kernel,
        in_specs=[IN_VMEM] * 2,
        out_specs=[IN_VMEM] * 5,
        out_shape=[pair_of, pair_of, pair_of, one_of, one_of],
        compiler_params=params,
        name="combine",
    )(keep_b, lax.ppermute(send_b, "col", SWAP_CORE))
    parts_a = lax.all_to_all(term_a, "row", 0, 0)
    four = lax.ppermute(four, "col", z_apart(2))
    three, one = (lax.ppermute(x, "col", z_apart(k)) for x, k in ((three, 3), (one, 1)))
    two = lax.ppermute(two.at[0].add(four), "col", z_apart(2))
    got = one + two + three
    other = lax.ppermute(got[1], "col", SWAP_CORE)

    grad_a, grad_b = pl.pallas_call(
        finish_kernel,
        in_specs=[IN_VMEM] * 4,
        out_specs=[IN_VMEM] * 2,
        out_shape=[
            jax.ShapeDtypeStruct((layers, RANKS_HERE, width), jnp.float32),
            jax.ShapeDtypeStruct((layers, RANKS_HERE, height), jnp.float32),
        ],
        compiler_params=params,
        name="finish",
    )(parts_a, here_b, got, other)
    return jnp.swapaxes(grad_b, 1, 2), grad_a, mags


def solution(mesh):
    in_specs = (
        P(None, "row", "col"),
        P(None, "row", "col"),
        P(None, "row", "col"),
        P(None, "row", "col"),
        P(None, "col"),
    )
    out_specs = (P(None, "row", "col"), P(None, "row", "col"), P(None, "col"))
    return jax.shard_map(
        on_device, mesh=mesh, in_specs=in_specs, out_specs=out_specs, check_vma=False
    )
```

```python
import jax
import jax.numpy as jnp
from jax import lax
from jax.experimental import pallas as pl
from jax.experimental.pallas import tpu as pltpu
from jax.sharding import PartitionSpec as P

epsilon = 1e-06
LAYERS = 2
GROUPS = 16
RANKS_HERE = 4
SLAB = LAYERS * RANKS_HERE
DEPTH = GROUPS * SLAB
SIDE = 4
RING = 8
REACH = RING // 2
BLOCK = 256
VMEM_BYTES = 20 * 1024 * 1024
IN_VMEM = pl.BlockSpec(memory_space=pltpu.VMEM)
ANYWHERE = pl.BlockSpec(memory_space=pl.ANY)
IN_SMEM = pl.BlockSpec(memory_space=pltpu.SMEM)

SWAP_CORE = [(i, i ^ 1) for i in range(GROUPS)]


def z_apart(k):
    ahead = [(2 * z, (z + k) % RING * 2) for z in range(RING)]
    behind = [(2 * z + 1, (z + RING - k) % RING * 2 + 1) for z in range(RING)]
    return ahead + behind


SEEN = [(1, 0), (1, 1), (2, 0), (2, 1), (3, 0), (3, 1), (REACH, 0), (0, 0)]


def row_shift(k, second):
    pairs = []
    for row in range(GROUPS):
        y, x = row // SIDE, row % SIDE
        for col in range(GROUPS):
            along_y = (col % 2 + second) % 2
            to = (y + k) % SIDE * SIDE + x if along_y else y * SIDE + (x + k) % SIDE
            pairs.append((row * GROUPS + col, to * GROUPS + col))
    return pairs


def col_group(col, core_sign, k, swap):
    core = col % 2
    step = core_sign * (1 - 2 * core) * k
    return (col // 2 + RING + step) % RING * 2 + (core + swap) % 2


def row_group(row, col, second, first):
    core = col % 2
    ky = second * (1 - core) + first * core
    kx = first * (1 - core) + second * core
    return (row // SIDE + SIDE - ky) % SIDE * SIDE + (row % SIDE + SIDE - kx) % SIDE


def row_place(row, col, group):
    core = col % 2
    ky = (row // SIDE + SIDE - group // SIDE) % SIDE
    kx = (row % SIDE + SIDE - group % SIDE) % SIDE
    return (ky * (1 - core) + kx * core) * SIDE + kx * (1 - core) + ky * core


def layer_mask(layer, shape):
    row = lax.broadcasted_iota(jnp.int32, shape, 0)
    return (row // RANKS_HERE) % LAYERS == layer


def fetch_kernel(up_hbm, other_ref, down_hbm, pair_ref, down_ref, sems):
    copies = [
        pltpu.make_async_copy(up_hbm, pair_ref.at[0], sems.at[0]),
        pltpu.make_async_copy(down_hbm, down_ref, sems.at[1]),
    ]
    for copy in copies:
        copy.start()
    pair_ref[1] = other_ref[...]
    for copy in copies:
        copy.wait()


def stack_kernel(d0, d1, d2, d3, out_ref):
    rows = [d[layer].astype(jnp.float32) for d in (d0, d1, d2, d3) for layer in range(LAYERS)]
    out_ref[...] = jnp.concatenate(rows, axis=0).astype(jnp.bfloat16)


def prepare_kernel(me_ref, pair, mine, theirs, bz_ref, bt_ref, found, order):
    row, col = me_ref[0], me_ref[1]

    def put(group, slab):
        for layer in range(LAYERS):
            found[group, layer * RANKS_HERE : (layer + 1) * RANKS_HERE, :] = slab[layer].astype(jnp.float32)

    for at, (k, swap) in enumerate(SEEN[:-1]):
        put(col_group(col, -1, k, swap), mine[at])
        put(col_group(col, 1, k, 1 - swap), theirs[at])
    for swap in range(2):
        put(col_group(col, 1, 0, swap), pair[swap])
    for second in range(SIDE):
        for first in range(SIDE):
            order[second * SIDE + first] = found[row_group(row, col, second, first)]
    here, there = (x[...].reshape(DEPTH, found.shape[2]) for x in (found, order))
    for layer in range(LAYERS):
        mask = layer_mask(layer, here.shape)
        span = pl.ds(layer * found.shape[2], found.shape[2])
        bz_ref[:, span] = jnp.where(mask, here, 0.0).astype(jnp.bfloat16)
        bt_ref[layer] = jnp.where(mask, there, 0.0).T.astype(jnp.bfloat16)


def sums_kernel(w_ref, g_ref, bt_ref, a0, a1, a2, a3, s_ref):
    for start in range(0, w_ref.shape[2], BLOCK):
        here = pl.ds(start, BLOCK)
        a = jnp.concatenate([x[:, here] for x in (a0, a1, a2, a3)], axis=0)
        rows = []
        for layer in range(LAYERS):
            merged = w_ref[layer, :, here].astype(jnp.float32) + jnp.dot(
                bt_ref[layer], a, preferred_element_type=jnp.float32
            )
            cot = g_ref[layer, :, here].astype(jnp.float32)
            rows.append(jnp.sum(merged * merged, axis=0, keepdims=True))
            rows.append(jnp.sum(cot * merged, axis=0, keepdims=True))
        sums = jnp.concatenate(rows, axis=0)
        s_ref[:, :, here] = jnp.broadcast_to(sums[None], (GROUPS, 2 * LAYERS, BLOCK))


def grads_kernel(
    me_ref, w_ref, g_ref, bz_ref, bt_ref, a0, a1, a2, a3, s_ref, mag_ref,
    ta_ref, keep_ref, send_ref, gmag_ref, total,
):
    for start in range(0, w_ref.shape[2], BLOCK):
        here = pl.ds(start, BLOCK)
        a = jnp.concatenate([x[:, here] for x in (a0, a1, a2, a3)], axis=0)
        a_wide = a.astype(jnp.float32)
        sums = jnp.sum(s_ref[:, :, here], axis=0)
        grads = []
        factors = []
        for layer in range(LAYERS):
            squares = sums[2 * layer : 2 * layer + 1]
            inner = sums[2 * layer + 1 : 2 * layer + 2]
            norm = jnp.sqrt(squares + epsilon)
            scale = mag_ref[layer : layer + 1, here] / norm
            shrink = scale * inner / (norm * norm)
            gmag_ref[layer : layer + 1, here] = inner / norm
            merged = w_ref[layer, :, here].astype(jnp.float32) + jnp.dot(
                bt_ref[layer], a, preferred_element_type=jnp.float32
            )
            cot = g_ref[layer, :, here].astype(jnp.float32)
            grad = (scale * cot - shrink * merged).astype(jnp.bfloat16)
            az = jnp.where(layer_mask(layer, a_wide.shape), a_wide, 0.0).astype(jnp.bfloat16)
            grads.append(grad)
            factors.append(az)
        term_a = jnp.dot(
            bz_ref[...], jnp.concatenate(grads, axis=0), preferred_element_type=jnp.float32
        )
        ta_ref[:, :, here] = term_a.reshape(GROUPS, SLAB, BLOCK)
        term_b = lax.dot_general(
            jnp.concatenate(factors, axis=1),
            jnp.concatenate(grads, axis=1),
            (((1,), (1,)), ((), ())),
            preferred_element_type=jnp.float32,
        )
        term_b = term_b.reshape(total.shape)
        if start == 0:
            total[...] = term_b
        else:
            total[...] += term_b
    row, col = me_ref[0], me_ref[1]

    def sum_for(group):
        return total[row_place(row, col, group)]

    for at, (k, swap) in enumerate(SEEN):
        keep_ref[at] = sum_for(col_group(col, 1, k, swap))
        send_ref[at] = sum_for(col_group(col, -1, k, 1 - swap))


def combine_kernel(keep_ref, got_ref, one_ref, two_ref, three_ref, four_ref, here_ref):
    for k, ref in enumerate((one_ref, two_ref, three_ref)):
        ref[...] = keep_ref[2 * k : 2 * k + 2] + got_ref[2 * k : 2 * k + 2]
    four_ref[...] = keep_ref[6] + got_ref[6]
    here_ref[...] = keep_ref[7] + got_ref[7]


def finish_kernel(parts_ref, here_ref, got_ref, other_ref, ga_ref, gb_ref):
    sum_a = jnp.sum(parts_ref[...], axis=0)
    sum_b = here_ref[...] + got_ref[0] + other_ref[...]
    for layer in range(LAYERS):
        rows = slice(layer * RANKS_HERE, (layer + 1) * RANKS_HERE)
        ga_ref[layer] = sum_a[rows]
        gb_ref[layer] = sum_b[rows]


def in_hbm(x):
    return pltpu.with_memory_space_constraint(x, pltpu.HBM)


def on_device(weight, cotangent, up, down, magnitude):
    layers, height, width = weight.shape
    me = jnp.stack([lax.axis_index("row"), lax.axis_index("col")]).astype(jnp.int32)
    params = pltpu.CompilerParams(vmem_limit_bytes=VMEM_BYTES)

    up = jnp.swapaxes(up, 1, 2)
    pair, own = pl.pallas_call(
        fetch_kernel,
        in_specs=[ANYWHERE, IN_VMEM, ANYWHERE],
        out_specs=[IN_VMEM] * 2,
        out_shape=[
            jax.ShapeDtypeStruct((2, *up.shape), up.dtype),
            jax.ShapeDtypeStruct(down.shape, down.dtype),
        ],
        scratch_shapes=[pltpu.SemaphoreType.DMA((2,))],
        compiler_params=params,
        name="fetch",
    )(in_hbm(up), lax.ppermute(up, "col", SWAP_CORE), in_hbm(down))
    two = lax.ppermute(pair, "col", z_apart(2))
    one, three = (lax.ppermute(pair, "col", z_apart(k)) for k in (1, 3))
    four = lax.ppermute(two[0], "col", z_apart(2))
    mine = jnp.concatenate([one, two, three, four[None]])
    theirs = lax.ppermute(mine, "col", SWAP_CORE)

    near = [own] + [lax.ppermute(down, ("row", "col"), row_shift(k, 0)) for k in range(1, SIDE)]
    near = pl.pallas_call(
        stack_kernel,
        in_specs=[IN_VMEM] * SIDE,
        out_specs=IN_VMEM,
        out_shape=jax.ShapeDtypeStruct((SIDE * SLAB, width), down.dtype),
        compiler_params=params,
        cost_estimate=pl.CostEstimate(flops=10**10, bytes_accessed=10**6, transcendentals=0),
        name="stack",
    )(*near)
    downs = [near] + [lax.ppermute(near, ("row", "col"), row_shift(k, 1)) for k in range(1, SIDE)]

    up_rows, up_columns = pl.pallas_call(
        prepare_kernel,
        in_specs=[IN_SMEM] + [IN_VMEM] * 3,
        out_specs=[IN_VMEM] * 2,
        out_shape=[
            jax.ShapeDtypeStruct((DEPTH, layers * height), jnp.bfloat16),
            jax.ShapeDtypeStruct((layers, height, DEPTH), jnp.bfloat16),
        ],
        scratch_shapes=[pltpu.VMEM((GROUPS, SLAB, height), jnp.float32)] * 2,
        compiler_params=params,
        name="prepare",
    )(me, pair, mine, theirs)

    sums = pl.pallas_call(
        sums_kernel,
        in_specs=[IN_VMEM] * 7,
        out_specs=IN_VMEM,
        out_shape=jax.ShapeDtypeStruct((GROUPS, 2 * layers, width), jnp.float32),
        compiler_params=params,
        name="column_sums",
    )(weight, cotangent, up_columns, *downs)

    sums_all = lax.all_to_all(sums, "row", 0, 0)

    term_a, keep_b, send_b, mags = pl.pallas_call(
        grads_kernel,
        in_specs=[IN_SMEM] + [IN_VMEM] * 10,
        out_specs=[IN_VMEM] * 4,
        out_shape=[
            jax.ShapeDtypeStruct((GROUPS, SLAB, width), jnp.float32),
            *[jax.ShapeDtypeStruct((len(SEEN), SLAB, height), jnp.float32)] * 2,
            jax.ShapeDtypeStruct((layers, width), jnp.float32),
        ],
        scratch_shapes=[pltpu.VMEM((GROUPS, SLAB, height), jnp.float32)],
        compiler_params=params,
        name="gradients",
    )(me, weight, cotangent, up_rows, up_columns, *downs, sums_all, magnitude)

    pair_of = jax.ShapeDtypeStruct((2, SLAB, height), jnp.float32)
    one_of = jax.ShapeDtypeStruct((SLAB, height), jnp.float32)
    one, two, three, four, here_b = pl.pallas_call(
        combine_kernel,
        in_specs=[IN_VMEM] * 2,
        out_specs=[IN_VMEM] * 5,
        out_shape=[pair_of, pair_of, pair_of, one_of, one_of],
        compiler_params=params,
        name="combine",
    )(keep_b, lax.ppermute(send_b, "col", SWAP_CORE))
    parts_a = lax.all_to_all(term_a, "row", 0, 0)
    four = lax.ppermute(four, "col", z_apart(2))
    three, one = (lax.ppermute(x, "col", z_apart(k)) for x, k in ((three, 3), (one, 1)))
    two = lax.ppermute(two.at[0].add(four), "col", z_apart(2))
    got = one + two + three
    other = lax.ppermute(got[1], "col", SWAP_CORE)

    grad_a, grad_b = pl.pallas_call(
        finish_kernel,
        in_specs=[IN_VMEM] * 4,
        out_specs=[IN_VMEM] * 2,
        out_shape=[
            jax.ShapeDtypeStruct((layers, RANKS_HERE, width), jnp.float32),
            jax.ShapeDtypeStruct((layers, RANKS_HERE, height), jnp.float32),
        ],
        compiler_params=params,
        name="finish",
    )(parts_a, here_b, got, other)
    return jnp.swapaxes(grad_b, 1, 2), grad_a, mags


def solution(mesh):
    in_specs = (
        P(None, "row", "col"),
        P(None, "row", "col"),
        P(None, "row", "col"),
        P(None, "row", "col"),
        P(None, "col"),
    )
    out_specs = (P(None, "row", "col"), P(None, "row", "col"), P(None, "col"))
    return jax.shard_map(
        on_device, mesh=mesh, in_specs=in_specs, out_specs=out_specs, check_vma=False
    )
```

```python
import jax
import jax.numpy as jnp
from jax import lax
from jax.experimental import pallas as pl
from jax.experimental.pallas import tpu as pltpu
from jax.sharding import PartitionSpec as P

epsilon = 1e-06
LAYERS = 2
GROUPS = 16
RANKS_HERE = 4
SLAB = LAYERS * RANKS_HERE
DEPTH = GROUPS * SLAB
SIDE = 4
RING = 8
REACH = RING // 2
BLOCK = 256
VMEM_BYTES = 20 * 1024 * 1024
IN_VMEM = pl.BlockSpec(memory_space=pltpu.VMEM)
ANYWHERE = pl.BlockSpec(memory_space=pl.ANY)
IN_SMEM = pl.BlockSpec(memory_space=pltpu.SMEM)

SWAP_CORE = [(i, i ^ 1) for i in range(GROUPS)]


def z_apart(k):
    ahead = [(2 * z, (z + k) % RING * 2) for z in range(RING)]
    behind = [(2 * z + 1, (z + RING - k) % RING * 2 + 1) for z in range(RING)]
    return ahead + behind


SEEN = [(1, 0), (1, 1), (2, 0), (2, 1), (3, 0), (3, 1), (REACH, 0), (0, 0)]


def row_shift(k, second):
    pairs = []
    for row in range(GROUPS):
        y, x = row // SIDE, row % SIDE
        for col in range(GROUPS):
            along_y = (col % 2 + second) % 2
            to = (y + k) % SIDE * SIDE + x if along_y else y * SIDE + (x + k) % SIDE
            pairs.append((row * GROUPS + col, to * GROUPS + col))
    return pairs


def col_group(col, core_sign, k, swap):
    core = col % 2
    step = core_sign * (1 - 2 * core) * k
    return (col // 2 + RING + step) % RING * 2 + (core + swap) % 2


def row_group(row, col, second, first):
    core = col % 2
    ky = second * (1 - core) + first * core
    kx = first * (1 - core) + second * core
    return (row // SIDE + SIDE - ky) % SIDE * SIDE + (row % SIDE + SIDE - kx) % SIDE


def row_place(row, col, group):
    core = col % 2
    ky = (row // SIDE + SIDE - group // SIDE) % SIDE
    kx = (row % SIDE + SIDE - group % SIDE) % SIDE
    return (ky * (1 - core) + kx * core) * SIDE + kx * (1 - core) + ky * core


def layer_mask(layer, shape):
    row = lax.broadcasted_iota(jnp.int32, shape, 0)
    return (row // RANKS_HERE) % LAYERS == layer


def fetch_kernel(up_hbm, down_hbm, up_ref, down_ref, sems):
    copies = [
        pltpu.make_async_copy(up_hbm, up_ref, sems.at[0]),
        pltpu.make_async_copy(down_hbm, down_ref, sems.at[1]),
    ]
    for copy in copies:
        copy.start()
    for copy in copies:
        copy.wait()


def stack_kernel(d0, d1, d2, d3, out_ref):
    rows = [d[layer].astype(jnp.float32) for d in (d0, d1, d2, d3) for layer in range(LAYERS)]
    out_ref[...] = jnp.concatenate(rows, axis=0).astype(jnp.bfloat16)


def prepare_kernel(me_ref, pair, mine, theirs, bz_ref, bt_ref, found, order):
    row, col = me_ref[0], me_ref[1]

    def put(group, slab):
        for layer in range(LAYERS):
            found[group, layer * RANKS_HERE : (layer + 1) * RANKS_HERE, :] = slab[layer].astype(jnp.float32)

    for at, (k, swap) in enumerate(SEEN[:-1]):
        put(col_group(col, -1, k, swap), mine[at])
        put(col_group(col, 1, k, 1 - swap), theirs[at])
    for swap in range(2):
        put(col_group(col, 1, 0, swap), pair[swap])
    for second in range(SIDE):
        for first in range(SIDE):
            order[second * SIDE + first] = found[row_group(row, col, second, first)]
    here, there = (x[...].reshape(DEPTH, found.shape[2]) for x in (found, order))
    for layer in range(LAYERS):
        mask = layer_mask(layer, here.shape)
        span = pl.ds(layer * found.shape[2], found.shape[2])
        bz_ref[:, span] = jnp.where(mask, here, 0.0).astype(jnp.bfloat16)
        bt_ref[layer] = jnp.where(mask, there, 0.0).T.astype(jnp.bfloat16)


def sums_kernel(w_ref, g_ref, bt_ref, a0, a1, a2, a3, s_ref):
    for start in range(0, w_ref.shape[2], BLOCK):
        here = pl.ds(start, BLOCK)
        a = jnp.concatenate([x[:, here] for x in (a0, a1, a2, a3)], axis=0)
        rows = []
        for layer in range(LAYERS):
            merged = w_ref[layer, :, here].astype(jnp.float32) + jnp.dot(
                bt_ref[layer], a, preferred_element_type=jnp.float32
            )
            cot = g_ref[layer, :, here].astype(jnp.float32)
            rows.append(jnp.sum(merged * merged, axis=0, keepdims=True))
            rows.append(jnp.sum(cot * merged, axis=0, keepdims=True))
        sums = jnp.concatenate(rows, axis=0)
        s_ref[:, :, here] = jnp.broadcast_to(sums[None], (GROUPS, 2 * LAYERS, BLOCK))


def grads_kernel(
    me_ref, w_ref, g_ref, bz_ref, bt_ref, a0, a1, a2, a3, s_ref, mag_ref,
    ta_ref, keep_ref, send_ref, gmag_ref, total,
):
    for start in range(0, w_ref.shape[2], BLOCK):
        here = pl.ds(start, BLOCK)
        a = jnp.concatenate([x[:, here] for x in (a0, a1, a2, a3)], axis=0)
        a_wide = a.astype(jnp.float32)
        sums = jnp.sum(s_ref[:, :, here], axis=0)
        grads = []
        factors = []
        for layer in range(LAYERS):
            squares = sums[2 * layer : 2 * layer + 1]
            inner = sums[2 * layer + 1 : 2 * layer + 2]
            norm = jnp.sqrt(squares + epsilon)
            scale = mag_ref[layer : layer + 1, here] / norm
            shrink = scale * inner / (norm * norm)
            gmag_ref[layer : layer + 1, here] = inner / norm
            merged = w_ref[layer, :, here].astype(jnp.float32) + jnp.dot(
                bt_ref[layer], a, preferred_element_type=jnp.float32
            )
            cot = g_ref[layer, :, here].astype(jnp.float32)
            grad = (scale * cot - shrink * merged).astype(jnp.bfloat16)
            az = jnp.where(layer_mask(layer, a_wide.shape), a_wide, 0.0).astype(jnp.bfloat16)
            grads.append(grad)
            factors.append(az)
        term_a = jnp.dot(
            bz_ref[...], jnp.concatenate(grads, axis=0), preferred_element_type=jnp.float32
        )
        ta_ref[:, :, here] = term_a.reshape(GROUPS, SLAB, BLOCK)
        part_b = [
            lax.dot_general(f, g, (((1,), (1,)), ((), ())), preferred_element_type=jnp.float32)
            for f, g in zip(factors, grads)
        ]
        term_b = part_b[0] + part_b[1]
        term_b = term_b.reshape(total.shape)
        if start == 0:
            total[...] = term_b
        else:
            total[...] += term_b
    row, col = me_ref[0], me_ref[1]

    def sum_for(group):
        return total[row_place(row, col, group)]

    for at, (k, swap) in enumerate(SEEN):
        keep_ref[at] = sum_for(col_group(col, 1, k, swap))
        send_ref[at] = sum_for(col_group(col, -1, k, 1 - swap))


def combine_kernel(keep_ref, got_ref, one_ref, two_ref, three_ref, four_ref, here_ref):
    for k, ref in enumerate((one_ref, two_ref, three_ref)):
        ref[...] = keep_ref[2 * k : 2 * k + 2] + got_ref[2 * k : 2 * k + 2]
    four_ref[...] = keep_ref[6] + got_ref[6]
    here_ref[...] = keep_ref[7] + got_ref[7]


def finish_kernel(parts_ref, here_ref, got_ref, other_ref, ga_ref, gb_ref):
    sum_a = jnp.sum(parts_ref[...], axis=0)
    sum_b = here_ref[...] + got_ref[0] + other_ref[...]
    for layer in range(LAYERS):
        rows = slice(layer * RANKS_HERE, (layer + 1) * RANKS_HERE)
        ga_ref[layer] = sum_a[rows]
        gb_ref[layer] = sum_b[rows]


def in_hbm(x):
    return pltpu.with_memory_space_constraint(x, pltpu.HBM)


def on_device(weight, cotangent, up, down, magnitude):
    layers, height, width = weight.shape
    me = jnp.stack([lax.axis_index("row"), lax.axis_index("col")]).astype(jnp.int32)
    params = pltpu.CompilerParams(vmem_limit_bytes=VMEM_BYTES)

    up = jnp.swapaxes(up, 1, 2)
    other = lax.ppermute(up, "col", SWAP_CORE)
    up, own = pl.pallas_call(
        fetch_kernel,
        in_specs=[ANYWHERE] * 2,
        out_specs=[IN_VMEM] * 2,
        out_shape=[
            jax.ShapeDtypeStruct(up.shape, up.dtype),
            jax.ShapeDtypeStruct(down.shape, down.dtype),
        ],
        scratch_shapes=[pltpu.SemaphoreType.DMA((2,))],
        compiler_params=params,
        name="fetch",
    )(in_hbm(up), in_hbm(down))
    pair = jnp.stack([up, other])
    two = lax.ppermute(pair, "col", z_apart(2))
    one, three = (lax.ppermute(pair, "col", z_apart(k)) for k in (1, 3))
    four = lax.ppermute(two[0], "col", z_apart(2))
    mine = jnp.concatenate([one, two, three, four[None]])
    theirs = lax.ppermute(mine, "col", SWAP_CORE)

    near = [own] + [lax.ppermute(down, ("row", "col"), row_shift(k, 0)) for k in range(1, SIDE)]
    near = pl.pallas_call(
        stack_kernel,
        in_specs=[IN_VMEM] * SIDE,
        out_specs=IN_VMEM,
        out_shape=jax.ShapeDtypeStruct((SIDE * SLAB, width), down.dtype),
        compiler_params=params,
        cost_estimate=pl.CostEstimate(flops=10**10, bytes_accessed=10**6, transcendentals=0),
        name="stack",
    )(*near)
    downs = [near] + [lax.ppermute(near, ("row", "col"), row_shift(k, 1)) for k in range(1, SIDE)]

    up_rows, up_columns = pl.pallas_call(
        prepare_kernel,
        in_specs=[IN_SMEM] + [IN_VMEM] * 3,
        out_specs=[IN_VMEM] * 2,
        out_shape=[
            jax.ShapeDtypeStruct((DEPTH, layers * height), jnp.bfloat16),
            jax.ShapeDtypeStruct((layers, height, DEPTH), jnp.bfloat16),
        ],
        scratch_shapes=[pltpu.VMEM((GROUPS, SLAB, height), jnp.float32)] * 2,
        compiler_params=params,
        name="prepare",
    )(me, pair, mine, theirs)

    sums = pl.pallas_call(
        sums_kernel,
        in_specs=[IN_VMEM] * 7,
        out_specs=IN_VMEM,
        out_shape=jax.ShapeDtypeStruct((GROUPS, 2 * layers, width), jnp.float32),
        compiler_params=params,
        name="column_sums",
    )(weight, cotangent, up_columns, *downs)

    sums_all = lax.all_to_all(sums, "row", 0, 0)

    term_a, keep_b, send_b, mags = pl.pallas_call(
        grads_kernel,
        in_specs=[IN_SMEM] + [IN_VMEM] * 10,
        out_specs=[IN_VMEM] * 4,
        out_shape=[
            jax.ShapeDtypeStruct((GROUPS, SLAB, width), jnp.float32),
            *[jax.ShapeDtypeStruct((len(SEEN), SLAB, height), jnp.float32)] * 2,
            jax.ShapeDtypeStruct((layers, width), jnp.float32),
        ],
        scratch_shapes=[pltpu.VMEM((GROUPS, SLAB, height), jnp.float32)],
        compiler_params=params,
        name="gradients",
    )(me, weight, cotangent, up_rows, up_columns, *downs, sums_all, magnitude)

    pair_of = jax.ShapeDtypeStruct((2, SLAB, height), jnp.float32)
    one_of = jax.ShapeDtypeStruct((SLAB, height), jnp.float32)
    one, two, three, four, here_b = pl.pallas_call(
        combine_kernel,
        in_specs=[IN_VMEM] * 2,
        out_specs=[IN_VMEM] * 5,
        out_shape=[pair_of, pair_of, pair_of, one_of, one_of],
        compiler_params=params,
        name="combine",
    )(keep_b, lax.ppermute(send_b, "col", SWAP_CORE))
    parts_a = lax.all_to_all(term_a, "row", 0, 0)
    four = lax.ppermute(four, "col", z_apart(2))
    three, one = (lax.ppermute(x, "col", z_apart(k)) for x, k in ((three, 3), (one, 1)))
    two = lax.ppermute(two.at[0].add(four), "col", z_apart(2))
    got = one + two + three
    other = lax.ppermute(got[1], "col", SWAP_CORE)

    grad_a, grad_b = pl.pallas_call(
        finish_kernel,
        in_specs=[IN_VMEM] * 4,
        out_specs=[IN_VMEM] * 2,
        out_shape=[
            jax.ShapeDtypeStruct((layers, RANKS_HERE, width), jnp.float32),
            jax.ShapeDtypeStruct((layers, RANKS_HERE, height), jnp.float32),
        ],
        compiler_params=params,
        name="finish",
    )(parts_a, here_b, got, other)
    return jnp.swapaxes(grad_b, 1, 2), grad_a, mags


def solution(mesh):
    in_specs = (
        P(None, "row", "col"),
        P(None, "row", "col"),
        P(None, "row", "col"),
        P(None, "row", "col"),
        P(None, "col"),
    )
    out_specs = (P(None, "row", "col"), P(None, "row", "col"), P(None, "col"))
    return jax.shard_map(
        on_device, mesh=mesh, in_specs=in_specs, out_specs=out_specs, check_vma=False
    )
```

```python
import jax
import jax.numpy as jnp
from jax import lax
from jax.experimental import pallas as pl
from jax.experimental.pallas import tpu as pltpu
from jax.sharding import PartitionSpec as P

epsilon = 1e-06
LAYERS = 2
GROUPS = 16
RANKS_HERE = 4
SLAB = LAYERS * RANKS_HERE
DEPTH = GROUPS * SLAB
SIDE = 4
RING = 8
REACH = RING // 2
BLOCK = 256
VMEM_BYTES = 28 * 1024 * 1024
IN_VMEM = pl.BlockSpec(memory_space=pltpu.VMEM)
ANYWHERE = pl.BlockSpec(memory_space=pl.ANY)
IN_SMEM = pl.BlockSpec(memory_space=pltpu.SMEM)

SWAP_CORE = [(i, i ^ 1) for i in range(GROUPS)]


def z_apart(k):
    ahead = [(2 * z, (z + k) % RING * 2) for z in range(RING)]
    behind = [(2 * z + 1, (z + RING - k) % RING * 2 + 1) for z in range(RING)]
    return ahead + behind


SEEN = [(1, 0), (1, 1), (2, 0), (2, 1), (3, 0), (3, 1), (REACH, 0), (0, 0)]


def row_shift(k, second):
    pairs = []
    for row in range(GROUPS):
        y, x = row // SIDE, row % SIDE
        for col in range(GROUPS):
            along_y = (col + 1 + second) % 2
            to = (y + k) % SIDE * SIDE + x if along_y else y * SIDE + (x + k) % SIDE
            pairs.append((row * GROUPS + col, to * GROUPS + col))
    return pairs


def col_group(col, core_sign, k, swap):
    core = col % 2
    step = core_sign * (1 - 2 * core) * k
    return (col // 2 + RING + step) % RING * 2 + (core + swap) % 2


def row_group(row, col, second, first):
    core = 1 - col % 2
    ky = second * (1 - core) + first * core
    kx = first * (1 - core) + second * core
    return (row // SIDE + SIDE - ky) % SIDE * SIDE + (row % SIDE + SIDE - kx) % SIDE


def row_place(row, col, group):
    core = 1 - col % 2
    ky = (row // SIDE + SIDE - group // SIDE) % SIDE
    kx = (row % SIDE + SIDE - group % SIDE) % SIDE
    return (ky * (1 - core) + kx * core) * SIDE + kx * (1 - core) + ky * core


def layer_mask(layer, shape):
    row = lax.broadcasted_iota(jnp.int32, shape, 0)
    return (row // RANKS_HERE) % LAYERS == layer


def fetch_kernel(up_hbm, down_hbm, up_ref, down_ref, sems):
    copies = [
        pltpu.make_async_copy(up_hbm, up_ref, sems.at[0]),
        pltpu.make_async_copy(down_hbm, down_ref, sems.at[1]),
    ]
    for copy in copies:
        copy.start()
    for copy in copies:
        copy.wait()


def stack_kernel(d0, d1, d2, d3, out_ref):
    rows = [d[layer].astype(jnp.float32) for d in (d0, d1, d2, d3) for layer in range(LAYERS)]
    out_ref[...] = jnp.concatenate(rows, axis=0).astype(jnp.bfloat16)


def prepare_kernel(me_ref, pair, mine, theirs, bz_ref, bt_ref, found, order):
    row, col = me_ref[0], me_ref[1]

    def put(group, slab):
        for layer in range(LAYERS):
            found[group, layer * RANKS_HERE : (layer + 1) * RANKS_HERE, :] = slab[layer].astype(jnp.float32)

    for at, (k, swap) in enumerate(SEEN[:-1]):
        put(col_group(col, -1, k, swap), mine[at])
        put(col_group(col, 1, k, 1 - swap), theirs[at])
    for swap in range(2):
        put(col_group(col, 1, 0, swap), pair[swap])
    for second in range(SIDE):
        for first in range(SIDE):
            order[second * SIDE + first] = found[row_group(row, col, second, first)]
    here, there = (x[...].reshape(DEPTH, found.shape[2]) for x in (found, order))
    for layer in range(LAYERS):
        mask = layer_mask(layer, here.shape)
        span = pl.ds(layer * found.shape[2], found.shape[2])
        bz_ref[:, span] = jnp.where(mask, here, 0.0).astype(jnp.bfloat16)
        bt_ref[layer] = jnp.where(mask, there, 0.0).T.astype(jnp.bfloat16)


def sums_kernel(w_ref, g_ref, bt_ref, a0, a1, a2, a3, s_ref, kept_ref, rest_ref):
    for start in range(0, w_ref.shape[2], BLOCK):
        here = pl.ds(start, BLOCK)
        a = jnp.concatenate([x[:, here] for x in (a0, a1, a2, a3)], axis=0)
        rows = []
        for layer in range(LAYERS):
            merged = w_ref[layer, :, here].astype(jnp.float32) + jnp.dot(
                bt_ref[layer], a, preferred_element_type=jnp.float32
            )
            if layer == 0:
                kept_ref[:, here] = merged
            else:
                rest_ref[:, here] = w_ref[layer, :, here]
            cot = g_ref[layer, :, here].astype(jnp.float32)
            rows.append(jnp.sum(merged * merged, axis=0, keepdims=True))
            rows.append(jnp.sum(cot * merged, axis=0, keepdims=True))
        sums = jnp.concatenate(rows, axis=0)
        s_ref[:, :, here] = jnp.broadcast_to(sums[None], (GROUPS, 2 * LAYERS, BLOCK))


def grads_kernel(
    me_ref, kept_ref, rest_ref, g_ref, bz_ref, bt_ref, a0, a1, a2, a3, s_ref, mag_ref,
    ta_ref, keep_ref, send_ref, gmag_ref, total,
):
    for start in range(0, g_ref.shape[2], BLOCK):
        here = pl.ds(start, BLOCK)
        a = jnp.concatenate([x[:, here] for x in (a0, a1, a2, a3)], axis=0)
        a_wide = a.astype(jnp.float32)
        sums = jnp.sum(s_ref[:, :, here], axis=0)
        grads = []
        factors = []
        for layer in range(LAYERS):
            squares = sums[2 * layer : 2 * layer + 1]
            inner = sums[2 * layer + 1 : 2 * layer + 2]
            norm = jnp.sqrt(squares + epsilon)
            scale = mag_ref[layer : layer + 1, here] / norm
            shrink = scale * inner / (norm * norm)
            gmag_ref[layer : layer + 1, here] = inner / norm
            if layer == 0:
                merged = kept_ref[:, here]
            else:
                merged = rest_ref[:, here].astype(jnp.float32) + jnp.dot(
                    bt_ref[layer], a, preferred_element_type=jnp.float32
                )
            cot = g_ref[layer, :, here].astype(jnp.float32)
            grad = (scale * cot - shrink * merged).astype(jnp.bfloat16)
            az = jnp.where(layer_mask(layer, a_wide.shape), a_wide, 0.0).astype(jnp.bfloat16)
            grads.append(grad)
            factors.append(az)
        term_a = jnp.dot(
            bz_ref[...], jnp.concatenate(grads, axis=0), preferred_element_type=jnp.float32
        )
        ta_ref[:, :, here] = term_a.reshape(GROUPS, SLAB, BLOCK)
        part_b = [
            lax.dot_general(f, g, (((1,), (1,)), ((), ())), preferred_element_type=jnp.float32)
            for f, g in zip(factors, grads)
        ]
        term_b = part_b[0] + part_b[1]
        term_b = term_b.reshape(total.shape)
        if start == 0:
            total[...] = term_b
        else:
            total[...] += term_b
    row, col = me_ref[0], me_ref[1]

    def sum_for(group):
        return total[row_place(row, col, group)]

    for at, (k, swap) in enumerate(SEEN):
        keep_ref[at] = sum_for(col_group(col, 1, k, swap))
        send_ref[at] = sum_for(col_group(col, -1, k, 1 - swap))


def combine_kernel(keep_ref, got_ref, one_ref, two_ref, three_ref, four_ref, here_ref):
    for k, ref in enumerate((one_ref, two_ref, three_ref)):
        ref[...] = keep_ref[2 * k : 2 * k + 2] + got_ref[2 * k : 2 * k + 2]
    four_ref[...] = keep_ref[6] + got_ref[6]
    here_ref[...] = keep_ref[7] + got_ref[7]


def finish_kernel(parts_ref, here_ref, got_ref, other_ref, ga_ref, gb_ref):
    sum_a = jnp.sum(parts_ref[...], axis=0)
    sum_b = here_ref[...] + got_ref[0] + other_ref[...]
    for layer in range(LAYERS):
        rows = slice(layer * RANKS_HERE, (layer + 1) * RANKS_HERE)
        ga_ref[layer] = sum_a[rows]
        gb_ref[layer] = sum_b[rows]


def in_hbm(x):
    return pltpu.with_memory_space_constraint(x, pltpu.HBM)


def on_device(weight, cotangent, up, down, magnitude):
    layers, height, width = weight.shape
    me = jnp.stack([lax.axis_index("row"), lax.axis_index("col")]).astype(jnp.int32)
    params = pltpu.CompilerParams(vmem_limit_bytes=VMEM_BYTES)

    up = jnp.swapaxes(up, 1, 2)
    other = lax.ppermute(up, "col", SWAP_CORE)
    up, own = pl.pallas_call(
        fetch_kernel,
        in_specs=[ANYWHERE] * 2,
        out_specs=[IN_VMEM] * 2,
        out_shape=[
            jax.ShapeDtypeStruct(up.shape, up.dtype),
            jax.ShapeDtypeStruct(down.shape, down.dtype),
        ],
        scratch_shapes=[pltpu.SemaphoreType.DMA((2,))],
        compiler_params=params,
        name="fetch",
    )(in_hbm(up), in_hbm(down))
    pair = jnp.stack([up, other])
    two = lax.ppermute(pair, "col", z_apart(2))
    one, three = (lax.ppermute(pair, "col", z_apart(k)) for k in (1, 3))
    four = lax.ppermute(two[0], "col", z_apart(2))
    mine = jnp.concatenate([one, two, three, four[None]])
    theirs = lax.ppermute(mine, "col", SWAP_CORE)

    near = [own] + [lax.ppermute(down, ("row", "col"), row_shift(k, 0)) for k in range(1, SIDE)]
    near = pl.pallas_call(
        stack_kernel,
        in_specs=[IN_VMEM] * SIDE,
        out_specs=IN_VMEM,
        out_shape=jax.ShapeDtypeStruct((SIDE * SLAB, width), down.dtype),
        compiler_params=params,
        cost_estimate=pl.CostEstimate(flops=10**10, bytes_accessed=10**6, transcendentals=0),
        name="stack",
    )(*near)
    downs = [near] + [lax.ppermute(near, ("row", "col"), row_shift(k, 1)) for k in range(1, SIDE)]

    up_rows, up_columns = pl.pallas_call(
        prepare_kernel,
        in_specs=[IN_SMEM] + [IN_VMEM] * 3,
        out_specs=[IN_VMEM] * 2,
        out_shape=[
            jax.ShapeDtypeStruct((DEPTH, layers * height), jnp.bfloat16),
            jax.ShapeDtypeStruct((layers, height, DEPTH), jnp.bfloat16),
        ],
        scratch_shapes=[pltpu.VMEM((GROUPS, SLAB, height), jnp.float32)] * 2,
        compiler_params=params,
        name="prepare",
    )(me, pair, mine, theirs)

    sums, kept, rest = pl.pallas_call(
        sums_kernel,
        in_specs=[IN_VMEM] * 7,
        out_specs=[IN_VMEM] * 3,
        out_shape=[
            jax.ShapeDtypeStruct((GROUPS, 2 * layers, width), jnp.float32),
            jax.ShapeDtypeStruct((height, width), jnp.float32),
            jax.ShapeDtypeStruct((height, width), weight.dtype),
        ],
        compiler_params=params,
        name="column_sums",
    )(weight, cotangent, up_columns, *downs)

    sums_all = lax.all_to_all(sums, "row", 0, 0)

    term_a, keep_b, send_b, mags = pl.pallas_call(
        grads_kernel,
        in_specs=[IN_SMEM] + [IN_VMEM] * 11,
        out_specs=[IN_VMEM] * 4,
        out_shape=[
            jax.ShapeDtypeStruct((GROUPS, SLAB, width), jnp.float32),
            *[jax.ShapeDtypeStruct((len(SEEN), SLAB, height), jnp.float32)] * 2,
            jax.ShapeDtypeStruct((layers, width), jnp.float32),
        ],
        scratch_shapes=[pltpu.VMEM((GROUPS, SLAB, height), jnp.float32)],
        compiler_params=params,
        name="gradients",
    )(me, kept, rest, cotangent, up_rows, up_columns, *downs, sums_all, magnitude)

    pair_of = jax.ShapeDtypeStruct((2, SLAB, height), jnp.float32)
    one_of = jax.ShapeDtypeStruct((SLAB, height), jnp.float32)
    one, two, three, four, here_b = pl.pallas_call(
        combine_kernel,
        in_specs=[IN_VMEM] * 2,
        out_specs=[IN_VMEM] * 5,
        out_shape=[pair_of, pair_of, pair_of, one_of, one_of],
        compiler_params=params,
        name="combine",
    )(keep_b, lax.ppermute(send_b, "col", SWAP_CORE))
    parts_a = lax.all_to_all(term_a, "row", 0, 0)
    four = lax.ppermute(four, "col", z_apart(2))
    three, one = (lax.ppermute(x, "col", z_apart(k)) for x, k in ((three, 3), (one, 1)))
    two = lax.ppermute(two.at[0].add(four), "col", z_apart(2))
    got = one + two + three
    other = lax.ppermute(got[1], "col", SWAP_CORE)

    grad_a, grad_b = pl.pallas_call(
        finish_kernel,
        in_specs=[IN_VMEM] * 4,
        out_specs=[IN_VMEM] * 2,
        out_shape=[
            jax.ShapeDtypeStruct((layers, RANKS_HERE, width), jnp.float32),
            jax.ShapeDtypeStruct((layers, RANKS_HERE, height), jnp.float32),
        ],
        compiler_params=params,
        name="finish",
    )(parts_a, here_b, got, other)
    return jnp.swapaxes(grad_b, 1, 2), grad_a, mags


def solution(mesh):
    in_specs = (
        P(None, "row", "col"),
        P(None, "row", "col"),
        P(None, "row", "col"),
        P(None, "row", "col"),
        P(None, "col"),
    )
    out_specs = (P(None, "row", "col"), P(None, "row", "col"), P(None, "col"))
    return jax.shard_map(
        on_device, mesh=mesh, in_specs=in_specs, out_specs=out_specs, check_vma=False
    )
```
